512 devices in a mesh: fsdp: 16 (over x_lo, y, core), ctx: 32 (over z, x_hi).
Axes of the slice: x: 4 (x_hi: 2, x_lo: 2; x = x_hi * 2 + x_lo), y: 4, z: 16, core: 2. Of those that a mesh axis runs over, the one named last changes fastest.
Arguments:
- tokens: bfloat16 [65536, 8192], P(('fsdp', 'ctx')), may hold values from -2000 to 2000
- doc_of_block: int32 [16, 32], P('fsdp'), may hold values from 0 to 7, never falling along the last dimension, each value on 1 to 17 neighbouring positions
- norm_gain: float32 [8192], replicated, may hold values from 0.1 to 3
- w_query: bfloat16 [8192, 512], P('fsdp'), may hold values from -1 to 1
- w_key: bfloat16 [8192, 128], P('fsdp'), may hold values from -1 to 1
- w_value: bfloat16 [8192, 128], P('fsdp'), may hold values from -0.0625 to 0.0625
Outputs:
- attended: bfloat16 [65536, 512], P(('fsdp', 'ctx'))
The draws below stay inside these ranges and needn't reach their ends.
Inputs may be any that keep to these rules, and one draw needn't show every extreme that they name: `doc_of_block`: along each row the numbers never fall; each document covers 1 to 17 whole blocks, one exactly 17.
All inputs are finite; a program needn't handle non-finite values.
Results may differ from the reference program's by a relative error of at most 0.0079.
Values may be sent and summed in bfloat16 or wider, within the bound.
A program may use at most 64 MiB of HBM per device.

```python
import math
import jax
import jax.numpy as jnp
import numpy as np
from jax import lax

D = 8192
HEAD = 128
QHEADS = 4
BLOCK = 128
TOK_DEV = 128
QH = 512
SEQ = 4096
TOKENS = 65536
NBLK = 32
DOCS = 8
MOST_BLK = 17
N_FSDP = 16


def draw_tokens(key, part):
    base_normal = jnp.clip(jax.random.normal(jax.random.fold_in(key, 1), (TOKENS, D), jnp.float32), -5.0, 5.0)
    row_scales = jnp.exp(jax.random.uniform(jax.random.fold_in(key, 2), (TOKENS, 1), jnp.float32, 0.0, math.log(10.0)))
    return (row_scales * base_normal).astype(jnp.bfloat16)


def draw_norm_gain(key, part):
    return jax.random.uniform(jax.random.fold_in(key, 7), (D,), jnp.float32, 0.5, 1.5)


def draw_w_query(key, part):
    independent = jnp.clip(jax.random.normal(jax.random.fold_in(key, 8), (D, QH), jnp.float32), -5.0, 5.0)
    return (independent * D ** (-0.5)).astype(jnp.bfloat16)


def draw_w_key(key, part):
    independent = jnp.clip(jax.random.normal(jax.random.fold_in(key, 9), (D, HEAD), jnp.float32), -5.0, 5.0)
    return (independent * D ** (-0.5)).astype(jnp.bfloat16)


def block_levels(rng, extent, cuts, smallest, top_value):
    def one(axis_at, blocks):
        steps = jax.random.uniform(jax.random.fold_in(jax.random.fold_in(rng, 6), axis_at), (blocks,), jnp.float32, smallest / len(cuts), top_value / len(cuts))
        return jnp.repeat(jnp.exp(steps), extent[axis_at] // blocks).reshape((-1,) + (1,) * (len(extent) - axis_at - 1))

    level = one(*cuts[0])
    for cut in cuts[1:]:
        level = level * one(*cut)
    return level


def profile(amount, total, reach, lean):
    weights = [(1 << 20) // math.isqrt(standing ** lean) + 1 for standing in range(2, amount + 1)]
    spare, given = total - reach - (amount - 1), [1] * (amount - 1)
    while spare > 0:
        candidates = [i for i in range(amount - 1) if given[i] < reach]
        whole, budget = sum([weights[i] for i in candidates]), spare
        for i in candidates:
            more = min(reach - given[i], max(1, budget * weights[i] // whole), spare)
            given[i] = given[i] + more
            spare = spare - more
    return np.array([reach] + given)


def ragged_sizes(key, number_of, total, limit, slope):
    if number_of == 2:
        one = jax.random.randint(key, (), max(1, total - limit), min(limit, total - 1) + 1)
        return jnp.stack([one, total - one])
    tallies = jnp.asarray(profile(number_of, total, limit, slope), jnp.int32)
    couples = (number_of - 1) // 2
    source_of, taker = tallies[1:1 + 2 * couples:2], tallies[2:2 + 2 * couples:2]
    slack = jnp.minimum(source_of - 1, limit - taker)
    shifted = jax.random.randint(jax.random.fold_in(key, 1), (couples,), 0, 1 << 20) % (slack + 1)
    tallies = tallies.at[1:1 + 2 * couples:2].set(source_of - shifted).at[2:2 + 2 * couples:2].set(taker + shifted)
    return tallies[jax.random.permutation(jax.random.fold_in(key, 2), number_of)]


def centred(own_key, dims, width, bound, shards=(), kind=jnp.bfloat16):
    factor_of = block_levels(own_key, dims, shards, -0.22, 0.18) if shards else 1.0
    values = jax.random.normal(own_key, dims, jnp.float32) * width * factor_of
    return jnp.minimum(jnp.maximum(values, -bound), bound).astype(kind)


def setup_inputs(seed: int = 0) -> dict:
    key_of = jax.random.split(jax.random.key(seed), 7)
    return {
        "tokens": draw_tokens(jax.random.fold_in(key_of[6], 71), 0),
        "doc_of_block": jax.vmap(lambda own: jnp.searchsorted(jnp.cumsum(ragged_sizes(own, DOCS, NBLK, MOST_BLK, 2)), jnp.arange(NBLK), side="right"))(jax.random.split(key_of[1], N_FSDP)).reshape((N_FSDP, NBLK)).astype(jnp.int32),
        "norm_gain": draw_norm_gain(jax.random.fold_in(key_of[6], 71), 0),
        "w_query": draw_w_query(jax.random.fold_in(key_of[6], 71), 0),
        "w_key": draw_w_key(jax.random.fold_in(key_of[6], 71), 0),
        "w_value": centred(key_of[5], (D, HEAD), D ** -0.5, 0.0625, ((0, 16),)),
    }


EPSILON = 1e-05
ROPE_BASE = 500000.0

def rotate(inputs, positions):
    half_size = inputs.shape[-1] // 2
    frequencies = ROPE_BASE ** (-2.0 * jnp.arange(half_size, dtype=jnp.float32) / inputs.shape[-1])
    angles = positions.astype(jnp.float32)[:, None] * frequencies[None, :]
    cosine = jnp.cos(angles)[:, None, :]
    sine_part = jnp.sin(angles)[:, None, :]
    first_half = inputs[..., :half_size]
    second_half = inputs[..., half_size:]
    return jnp.concatenate([first_half * cosine - second_half * sine_part, second_half * cosine + first_half * sine_part], -1)

def normalize(inputs, gain_vector):
    as_float = inputs.astype(jnp.float32)
    mean_square = lax.optimization_barrier(jnp.mean(as_float * as_float, -1, keepdims=True))
    return (as_float * lax.rsqrt(mean_square + EPSILON) * gain_vector).astype(jnp.bfloat16)

def reference(tokens, doc_of_block, norm_gain, w_query, w_key, w_value):
    sequences = tokens.reshape(N_FSDP, SEQ, D)

    def one_sequence(sequence_args):
        seq_rows, doc_table = sequence_args
        normed = normalize(seq_rows, norm_gain)
        positions = jnp.arange(SEQ, dtype=jnp.int32)
        query_rows = jnp.dot(normed, w_query, preferred_element_type=jnp.float32).reshape(SEQ, QHEADS, HEAD)
        query_rows = rotate(query_rows, positions).astype(jnp.bfloat16)
        key_rows = jnp.dot(normed, w_key, preferred_element_type=jnp.float32)[:, None, :]
        key_rows = rotate(key_rows, positions)[:, 0, :].astype(jnp.bfloat16)
        value_rows = jnp.dot(normed, w_value, preferred_element_type=jnp.float32).astype(jnp.bfloat16)
        token_docs = doc_table[positions // BLOCK]
        key_float = key_rows.astype(jnp.float32)
        value_float = value_rows.astype(jnp.float32)

        def attend_block(block_index):
            block_start = (block_index * TOK_DEV).astype(jnp.int32)
            query_block = lax.dynamic_slice_in_dim(query_rows, block_start, TOK_DEV, 0).astype(jnp.float32)
            query_position = block_start + jnp.arange(TOK_DEV, dtype=jnp.int32)
            query_doc = lax.dynamic_slice_in_dim(token_docs, block_start, TOK_DEV, 0)
            scores = jnp.einsum('tgd,sd->gts', query_block, key_float) / math.sqrt(HEAD)
            allowed = (query_doc[:, None] == token_docs[None, :]) & (positions[None, :] <= query_position[:, None])
            scores = jnp.where(allowed[None], scores, -1e+30)
            row_max = lax.optimization_barrier(jnp.max(scores, -1, keepdims=True))
            weights = jnp.where(allowed[None], jnp.exp(scores - row_max), 0.0)
            row_sum = lax.optimization_barrier(jnp.sum(weights, -1))
            rounded = lax.optimization_barrier(weights.astype(jnp.bfloat16))
            weighted = jnp.einsum('gts,sd->gtd', rounded.astype(jnp.float32), value_float)
            result = (weighted / row_sum[..., None]).astype(jnp.bfloat16)
            return result.transpose(1, 0, 2).reshape(TOK_DEV, QH)
        pieces = lax.map(attend_block, jnp.arange(SEQ // TOK_DEV, dtype=jnp.int32))
        return pieces.reshape(SEQ, QH)
    return lax.map(one_sequence, (sequences, doc_of_block)).reshape(TOKENS, QH)
```

```python
import functools
import math

import jax
import jax.numpy as jnp
import numpy as np
from jax import lax
from jax.experimental import pallas as pl
from jax.experimental.pallas import tpu as pltpu
from jax.sharding import PartitionSpec as P

BLOCK = 128
EPSILON = 1e-05
ROPE_BASE = 500000.0
NEG = -1e30
MESH = pl.DeviceIdType.MESH

EDGES = ((0, 3), (0, 1), (3, 6), (3, 4), (3, 2), (6, 8), (6, 7), (6, 5))
REACH = 8
GROUPS = ((0, 4), (4, 7), (7, 9))


def tables(blocks, head):
    half = head // 2
    freq = (ROPE_BASE ** (-2.0 * np.arange(half, dtype=np.float64) / head)).astype(np.float32).astype(np.float64)
    freq = np.concatenate([freq, freq])[None, :]
    inner = np.arange(BLOCK, dtype=np.float64)[:, None] * freq
    outer = np.arange(blocks, dtype=np.float64)[:, None] * BLOCK * freq
    return [t.astype(np.float32) for t in (np.cos(inner), np.sin(inner), np.cos(outer), np.sin(outer))]


def kernel(
    tok, gain, wq_in, wk_in, wv_in, cos_in, sin_in, cos_out, sin_out, doc, out,
    xbuf, tbuf, wkv, wq, kvb, pf_kv, pr_kv, pf_q, pr_q, qs,
    tok_s, tok_r, wy_s, wy_r, wc_s, wc_r, pp_s, pp_r, z_s, z_r, xp_s, xp_r,
):
    f = lax.axis_index("fsdp")
    ctx = lax.axis_index("ctx")
    xl, y, c = f // 8, (f // 2) % 4, f % 2
    z, xh = ctx // 2, ctx % 2
    x = xh * 2 + xl

    def at_x(nx):
        nx = nx % 4
        return {"fsdp": (nx % 2) * 8 + y * 2 + c, "ctx": z * 2 + nx // 2}

    def at_y(ny):
        return {"fsdp": xl * 8 + (ny % 4) * 2 + c, "ctx": ctx}

    def at_z(nz):
        return {"fsdp": f, "ctx": (nz % 16) * 2 + xh}

    sib = {"fsdp": xl * 8 + y * 2 + (1 - c), "ctx": ctx}
    ahead, behind = at_x(x + 5 - 2 * c), at_x(x + 3 + 2 * c)
    partner = at_x(x + 2)
    ys = (y + 1, y + 3, y + 2)

    barrier = pltpu.get_barrier_semaphore()
    friends = [ahead, behind, partner, sib] + [at_y(v) for v in ys]
    friends += [at_z(z + d) for d in (1, 15, 2, 14, 3, 13)]
    for who in friends:
        pl.semaphore_signal(barrier, inc=1, device_id=who, device_id_type=MESH)

    def remote(src, dst, send, recv, who):
        return pltpu.make_async_remote_copy(
            src_ref=src, dst_ref=dst, send_sem=send, recv_sem=recv, device_id=who, device_id_type=MESH
        )

    mine = y * 2 + c
    def add_square(j, acc):
        v = tok[:, pl.ds(pl.multiple_of(j * 512, 512), 512)].astype(jnp.float32)
        v = v * v
        return acc + (v[:, :128] + v[:, 128:256]) + (v[:, 256:384] + v[:, 384:])

    total = lax.fori_loop(0, 16, add_square, jnp.zeros((BLOCK, 128), jnp.float32))
    scale = lax.rsqrt(jnp.sum(total, axis=1, keepdims=True) / 8192.0 + EPSILON)

    def norm_slot(s, carry):
        for other in (1, 0):
            group = xl if other == 0 else 1 - xl
            cols = pl.ds(pl.multiple_of(group * 4096 + s * 512, 512), 512)
            v = (tok[:, cols].astype(jnp.float32) * scale * gain[:, cols]).astype(jnp.bfloat16)
            if other:
                tbuf[s] = v
            else:
                xbuf[s, 0:128, :] = v
        return carry

    lax.fori_loop(0, 8, norm_slot, 0)
    wkv[mine, :, 0:128] = wk_in[...]
    wkv[mine, :, 128:256] = wv_in[...]
    wq[mine] = wq_in[...]

    pl.semaphore_wait(barrier, len(friends))

    toks = [
        remote(tbuf.at[s], xbuf.at[s, pl.ds(128, 128)], tok_s.at[s], tok_r.at[s], ahead) for s in range(8)
    ]
    wkv_y = [remote(wkv.at[mine], wkv.at[mine], wy_s.at[i], wy_r.at[i], at_y(ys[i])) for i in range(3)]
    wq_y = [remote(wq.at[mine], wq.at[mine], wy_s.at[3 + i], wy_r.at[3 + i], at_y(ys[i])) for i in range(3)]
    froms = [((y + 3) % 4) * 2 + c, ((y + 1) % 4) * 2 + c, ((y + 2) % 4) * 2 + c]
    wkv_in = [remote(wkv.at[s], wkv.at[s], wy_s.at[i], wy_r.at[i], at_y(ys[i])) for i, s in enumerate(froms)]
    wq_got = [remote(wq.at[s], wq.at[s], wy_s.at[3 + i], wy_r.at[3 + i], at_y(ys[i])) for i, s in enumerate(froms)]
    held = [mine] + froms

    def to_sibling(buf, base, i):
        return remote(buf.at[held[i]], buf.at[held[i]], wc_s.at[base + i], wc_r.at[base + i], sib)

    def from_sibling(buf, base, i):
        s = held[i] + 1 - 2 * c
        return remote(buf.at[s], buf.at[s], wc_s.at[base + i], wc_r.at[base + i], sib)

    for i in range(3):
        wkv_y[i].start()
    for t in toks:
        t.start()
    to_sibling(wkv, 0, 0).start()
    to_sibling(wq, 4, 0).start()
    for i in range(3):
        wkv_y[i].wait_send()
    for i in range(3):
        wq_y[i].start()
    for i in range(3):
        wkv_in[i].wait_recv()
        to_sibling(wkv, 0, 1 + i).start()
    for i in range(4):
        from_sibling(wkv, 0, i).wait_recv()
    for t in toks:
        t.wait_recv()

    def project(buf, width):
        def step(s, acc):
            return acc + jnp.dot(xbuf[s], buf[s], preferred_element_type=jnp.float32)

        return lax.fori_loop(0, 8, step, jnp.zeros((256, width), jnp.float32))

    acc = project(wkv, 256)
    pf_kv[...] = acc[128:]
    back_kv = remote(pf_kv, pr_kv, pp_s.at[0], pp_r.at[0], behind)
    back_kv.start()
    co, so = cos_out[pl.ds(ctx, 1), :], sin_out[pl.ds(ctx, 1), :]
    cosine = co * cos_in[...] - so * sin_in[...]
    sine = so * cos_in[...] + co * sin_in[...]
    lane = lax.broadcasted_iota(jnp.int32, (BLOCK, 128), 1)
    sine = jnp.where(lane < 64, -sine, sine)

    def rotate(v):
        return (v * cosine + pltpu.roll(v, 64, 1) * sine).astype(jnp.bfloat16)

    back_kv.wait_recv()
    own = acc[:128] + pr_kv[...]
    kvb[0, 0, :, 0:128] = rotate(own[:, :128])
    kvb[0, 0, :, 128:256] = own[:, 128:].astype(jnp.bfloat16)

    edges = {
        (a, b): remote(kvb.at[0, a], kvb.at[0, b], z_s.at[b - 1], z_r.at[b - 1], at_z(z + b - a + 16))
        for a, b in EDGES
    }
    across = [remote(kvb.at[0, d], kvb.at[1, d], xp_s.at[d], xp_r.at[d], partner) for d in range(REACH + 1)]

    def pass_on(d):
        if d:
            edges[next(e for e in EDGES if e[1] == d)].wait_recv()
        for a, b in EDGES:
            if a == d:
                edges[(a, b)].start()
        across[d].start()

    for d in (0, 3, 1, 6, 2, 4):
        pass_on(d)
    for i in range(3):
        wq_got[i].wait_recv()
        to_sibling(wq, 4, 1 + i).start()
    for i in range(4):
        from_sibling(wq, 4, i).wait_recv()
    acc_q = project(wq, 512)
    pf_q[...] = acc_q[128:]
    back_q = remote(pf_q, pr_q, pp_s.at[1], pp_r.at[1], behind)
    back_q.start()
    for d in (5, 7, 8):
        pass_on(d)
    back_q.wait_recv()
    for h in range(4):
        cols = slice(h * 128, (h + 1) * 128)
        qs[cols, :] = rotate(acc_q[:128, cols] + pr_q[:, cols])

    my_doc = doc[0, ctx]

    def bias_of(block):
        ok = (block >= 0) & (block <= ctx) & (doc[0, jnp.clip(block, 0, 31)] == my_doc)
        return jnp.where(ok, 0.0, NEG).astype(jnp.float32)

    row = lax.broadcasted_iota(jnp.int32, (512, 128), 0) % BLOCK
    col = lax.broadcasted_iota(jnp.int32, (512, 128), 1)
    triangle = jnp.where(col <= row, 0.0, NEG)
    state = None
    for first, last in GROUPS:
        n = last - first
        for d in range(first, last):
            across[d].wait_recv()
        keys = kvb[:, first:last, :, 0:128].reshape(2 * n * BLOCK, 128)
        vals = kvb[:, first:last, :, 128:256].reshape(2 * n * BLOCK, 128)
        scores = lax.dot_general(qs[...], keys, (((1,), (1,)), ((), ())), preferred_element_type=jnp.float32)
        bias = jnp.concatenate(
            [
                jnp.full((1, BLOCK), bias_of(ctx - 2 * d + lane_at * (1 - 2 * xh)), jnp.float32)
                for lane_at in (0, 1)
                for d in range(first, last)
            ],
            axis=1,
        )
        scores = scores * (1.0 / math.sqrt(128.0)) + bias
        if first == 0:
            scores = jnp.concatenate([scores[:, :128] + triangle, scores[:, 128:]], axis=1)
        top = jnp.max(scores, axis=1, keepdims=True)
        if state is not None:
            top = jnp.maximum(state[0], top)
        weights = jnp.exp(scores - top)
        sums = jnp.sum(weights, axis=1, keepdims=True)
        outs = jnp.dot(weights.astype(jnp.bfloat16), vals, preferred_element_type=jnp.float32)
        if state is not None:
            decay = jnp.exp(state[0] - top)
            sums, outs = sums + state[1] * decay, outs + state[2] * decay
        state = (top, sums, outs)
    result = (state[2] / state[1]).astype(jnp.bfloat16)
    for h in range(4):
        out[:, h * 128 : (h + 1) * 128] = result[h * 128 : (h + 1) * 128, :]

    for copy in toks + wq_y + [back_kv, back_q] + across + [edges[e] for e in EDGES]:
        copy.wait_send()
    for i in range(4):
        to_sibling(wkv, 0, i).wait_send()
        to_sibling(wq, 4, i).wait_send()


def body(tokens, doc_of_block, norm_gain, w_query, w_key, w_value):
    vmem, smem = pl.BlockSpec(memory_space=pltpu.VMEM), pl.BlockSpec(memory_space=pltpu.SMEM)
    dma = pltpu.SemaphoreType.DMA
    bf, fl = jnp.bfloat16, jnp.float32
    return pl.pallas_call(
        kernel,
        out_shape=jax.ShapeDtypeStruct((128, 512), bf),
        in_specs=[vmem] * 9 + [smem],
        out_specs=vmem,
        scratch_shapes=[
            pltpu.VMEM((8, 256, 512), bf),
            pltpu.VMEM((8, 128, 512), bf),
            pltpu.VMEM((8, 512, 256), bf),
            pltpu.VMEM((8, 512, 512), bf),
            pltpu.VMEM((2, REACH + 1, 128, 256), bf),
            pltpu.VMEM((128, 256), fl),
            pltpu.VMEM((128, 256), fl),
            pltpu.VMEM((128, 512), fl),
            pltpu.VMEM((128, 512), fl),
            pltpu.VMEM((512, 128), bf),
            dma((8,)), dma((8,)),
            dma((6,)), dma((6,)),
            dma((8,)), dma((8,)),
            dma((2,)), dma((2,)),
            dma((REACH,)), dma((REACH,)),
            dma((REACH + 1,)), dma((REACH + 1,)),
        ],
        compiler_params=pltpu.CompilerParams(
            collective_id=0, has_side_effects=True, vmem_limit_bytes=48 * 2**20
        ),
    )(
        tokens, norm_gain.reshape(1, -1), w_query, w_key, w_value,
        *[jnp.asarray(t) for t in tables(32, 128)], doc_of_block,
    )


def solution(mesh):
    placed = (
        P(("fsdp", "ctx"), None),
        P("fsdp", None),
        P(),
        P("fsdp", None),
        P("fsdp", None),
        P("fsdp", None),
    )
    return jax.shard_map(
        body, mesh=mesh, in_specs=placed, out_specs=P(("fsdp", "ctx"), None), check_vma=False
    )
```
